128 devices in a mesh: group: 4 (over x_hi, core), replica: 32 (over x_lo, z, y).
Axes of the slice: x: 4 (x_hi: 2, x_lo: 2; x = x_hi * 2 + x_lo), y: 4, z: 4, core: 2. Of those that a mesh axis runs over, the one named last changes fastest.
Arguments:
- incoming_activations: bfloat16 [16384, 1152], P(('replica', 'group')), may hold values from -24 to 24
- document_offsets: int32 [16384], P('replica'), may hold values from 0 to 1999, as said below
- before_mixing_gain: float32 [1152], replicated, may hold values from 0.25 to 1.75
- asking_matrix: bfloat16 [1152, 1024], P(None, 'group'), may hold values from -0.1875 to 0.1875
- lookup_matrix: bfloat16 [1152, 256], replicated, may hold values from -0.1875 to 0.1875
- content_matrix: bfloat16 [1152, 256], replicated, may hold values from -0.1875 to 0.1875
- asking_norm_gain: float32 [256], replicated, may hold values from 1 to 2
- lookup_norm_gain: float32 [256], replicated, may hold values from 1 to 2
- mixing_matrix: bfloat16 [1024, 1152], P('group'), may hold values from -0.1875 to 0.1875
- after_mixing_gain: float32 [1152], replicated, may hold values from 0.25 to 1.75
- before_hidden_gain: float32 [1152], replicated, may hold values from 0.25 to 1.75
- gating_matrix_entries: bfloat16 [1152, 6912], P(None, 'group'), may hold values from -0.1875 to 0.1875
- widening_matrix: bfloat16 [1152, 6912], P(None, 'group'), may hold values from -0.1875 to 0.1875
- lowering_matrix: bfloat16 [6912, 1152], P('group'), may hold values from -0.078125 to 0.078125
- after_hidden_gain: float32 [1152], replicated, may hold values from 0.25 to 1.75
- loss_sensitivity: bfloat16 [16384, 1152], P(('replica', 'group')), may hold values from -24 to 24
Outputs:
- block_out: float32 [16384, 1152], P(('replica', 'group'))
- tokens_grad: float32 [16384, 1152], P(('replica', 'group'))
- entry_grad: float32 [1152], P(('group', 'replica'))
- query_grad: float32 [1152, 1024], P('replica', 'group')
- key_grad: float32 [1152, 256], P(('group', 'replica'))
- value_grad: float32 [1152, 256], P(('group', 'replica'))
- qscale_grad: float32 [256], P(('group', 'replica'))
- kscale_grad: float32 [256], P(('group', 'replica'))
- out_grad: float32 [1024, 1152], P('group', 'replica')
- attend_grad: float32 [1152], P(('group', 'replica'))
- inner_grad: float32 [1152], P(('group', 'replica'))
- gate_grad: float32 [1152, 6912], P('replica', 'group')
- up_grad: float32 [1152, 6912], P('replica', 'group')
- down_grad: float32 [6912, 1152], P('group', 'replica')
- closing_grad: float32 [1152], P(('group', 'replica'))
The draws below stay inside these ranges and needn't reach their ends.
Inputs may be any that keep to these rules, and one draw needn't show every extreme that they name: `document_offsets`: documents of 200 to 2000 tokens lie end to end over all 16384 tokens, the first of exactly 2000 tokens, the last possibly cut short; a position is 0 at a document's first token and rises by one with each further token.
All inputs are finite; a program needn't handle non-finite values.
Results may differ from the reference program's by a relative error of at most 0.035.
Values may be sent and summed in bfloat16 or wider, within the bound.
No kernel may reach another device: no remote copies, remote signals or barrier semaphores. Data moves between devices by JAX's collectives and lax.ppermute only.
A program may use at most 128 MiB of HBM per device.

```python
from functools import partial
import jax
import jax.numpy as jnp
from jax import lax

D = 1152
HEADS = 4
CHANNEL_COUNT = 256
FF = 6912
WINDOW = 512
DOC_MIN = 200
DOC_MAX = 2000
TOK_REP = 512
TOKENS = 16384


def draw_document_offsets(key, part):
    key = jax.random.fold_in(key, 11)
    doc_count = TOKENS // DOC_MIN + 2
    lengths = jax.random.randint(key, (doc_count,), DOC_MIN, DOC_MAX + 1, dtype=jnp.int32)
    lengths = lengths.at[0].set(DOC_MAX)
    doc_ends = jnp.cumsum(lengths).astype(jnp.int32)
    starts = doc_ends - lengths
    places = jnp.arange(TOKENS, dtype=jnp.int32)
    owners = jnp.sum((places[:, None] >= doc_ends[None, :]).astype(jnp.int32), axis=1)
    return places - jnp.take(starts, owners)


def with_spikes(drawn, own_key, source, target, parts, factor):
    owner, partner = [(jnp.arange(drawn.shape[position]) // (drawn.shape[position] // parts)).reshape([-1 if axis == position else 1 for axis in range(drawn.ndim)]) for position in (source, target)]
    chosen = jax.random.permutation(own_key, parts)[partner]
    strong = (owner == chosen) | (owner == (partner + parts // 2) % parts)
    return jnp.where(strong, factor * drawn, drawn)


def level_of(rng, shape, cuts, low, high):
    def one(axis_at, blocks):
        heights = jax.random.uniform(jax.random.fold_in(jax.random.fold_in(rng, 6), axis_at), (blocks,), jnp.float32, low / len(cuts), high / len(cuts))
        return jnp.repeat(jnp.exp(heights), shape[axis_at] // blocks).reshape((-1,) + (1,) * (len(shape) - axis_at - 1))

    gain = one(*cuts[0])
    for cut in cuts[1:]:
        gain = gain * one(*cut)
    return gain


def normal_values(own_key, dims, deviation, limit, shards=(), kind=jnp.bfloat16):
    loudness = level_of(own_key, dims, shards, -0.22, 0.18) if shards else 1.0
    values = jax.random.normal(own_key, dims, jnp.float32) * deviation * loudness
    return jnp.minimum(jnp.maximum(values, -limit), limit).astype(kind)


def noise_with(own_key, extent, deviation, bound, cuts, heavy, kind=jnp.bfloat16):
    drawn = deviation * jax.random.normal(own_key, extent, jnp.float32)
    if cuts:
        drawn = drawn * level_of(own_key, extent, cuts, -0.22, 0.18)
    return jnp.clip(with_spikes(drawn, jax.random.fold_in(own_key, 3), *heavy), -bound, bound).astype(kind)


def setup_inputs(seed: int = 0) -> dict:
    key_list = jax.random.split(jax.random.key(seed), 17)
    return {
        "incoming_activations": noise_with(key_list[0], (TOKENS, D), 1.0, 24.0, ((0, 128),), (0, 1, 128, 5.5)),
        "document_offsets": draw_document_offsets(jax.random.fold_in(key_list[16], 71), 0),
        "before_mixing_gain": jnp.clip(1.0 + 0.15 * jax.random.normal(key_list[2], (D,), jnp.float32), 0.25, 1.75),
        "asking_matrix": normal_values(key_list[3], (D, HEADS * CHANNEL_COUNT), D ** -0.5, 0.1875, ((1, 4),)),
        "lookup_matrix": normal_values(key_list[4], (D, CHANNEL_COUNT), D ** -0.5, 0.1875),
        "content_matrix": normal_values(key_list[5], (D, CHANNEL_COUNT), D ** -0.5, 0.1875),
        "asking_norm_gain": jnp.clip(jax.random.uniform(key_list[6], (CHANNEL_COUNT,), jnp.float32, 1.0, 2.0), 1.0, 2.0),
        "lookup_norm_gain": jnp.clip(jax.random.uniform(key_list[7], (CHANNEL_COUNT,), jnp.float32, 1.0, 2.0), 1.0, 2.0),
        "mixing_matrix": normal_values(key_list[8], (HEADS * CHANNEL_COUNT, D), (HEADS * CHANNEL_COUNT) ** -0.5, 0.1875, ((0, 4),)),
        "after_mixing_gain": jnp.clip(1.0 + 0.15 * jax.random.normal(key_list[9], (D,), jnp.float32), 0.25, 1.75),
        "before_hidden_gain": jnp.clip(1.0 + 0.15 * jax.random.normal(key_list[10], (D,), jnp.float32), 0.25, 1.75),
        "gating_matrix_entries": normal_values(key_list[11], (D, FF), D ** -0.5, 0.1875, ((1, 4),)),
        "widening_matrix": normal_values(key_list[12], (D, FF), D ** -0.5, 0.1875, ((1, 4),)),
        "lowering_matrix": normal_values(key_list[13], (FF, D), FF ** -0.5, 0.078125, ((0, 4),)),
        "after_hidden_gain": jnp.clip(1.0 + 0.15 * jax.random.normal(key_list[14], (D,), jnp.float32), 0.25, 1.75),
        "loss_sensitivity": noise_with(key_list[15], (TOKENS, D), 1.0, 24.0, ((0, 128),), (0, 1, 128, 5.5)),
    }


@jax.custom_vjp
def narrow_number_format(v):
    return lax.optimization_barrier(v.astype(jnp.bfloat16)).astype(jnp.float32)

@jax.custom_vjp
def low_back(v):
    return v

def low_keep(v):
    return (narrow_number_format(v), None)

def low_pass(kept, grad):
    return (grad,)

def back_keep(v):
    return (v, None)

def back_low(kept, grad):
    return (narrow_number_format(grad),)
narrow_number_format.defvjp(low_keep, low_pass)
low_back.defvjp(back_keep, back_low)
highest = lax.Precision.HIGHEST
epsilon = 1e-06
big_negative = -1e+30

def quadratic_norm_apply(values, scaling):
    return values * lax.rsqrt(lax.optimization_barrier(jnp.mean(values * values, axis=-1, keepdims=True)) + epsilon) * scaling

def angular_position_turn(values, places):
    halfway = values.shape[-1] // 2
    inverse = 10000.0 ** (-2.0 * jnp.arange(halfway, dtype=jnp.float32) / values.shape[-1])
    angles = places.astype(jnp.float32)[:, None] * inverse[None, :]
    cosine = jnp.cos(angles)
    sine_of = jnp.sin(angles)
    former = values[..., :halfway]
    latter = values[..., halfway:]
    return jnp.concatenate([former * cosine - latter * sine_of, latter * cosine + former * sine_of], axis=-1)

def allowed_pairs(query_index, key_index, starts):
    return (key_index[None, :] <= query_index[:, None]) & (key_index[None, :] > query_index[:, None] - WINDOW) & (key_index[None, :] >= starts[:, None])

def feed_block(row_block, gating_matrix_entries, widening_matrix, lowering_matrix):
    gating = low_back(jnp.dot(row_block, gating_matrix_entries, precision=highest))
    upward = low_back(jnp.dot(row_block, widening_matrix, precision=highest))
    active = narrow_number_format(jax.nn.gelu(gating, approximate=True) * upward)
    return jnp.dot(active, lowering_matrix, precision=highest)

def complete_decoder_block(incoming_activations, before_mixing_gain, asking_matrix, lookup_matrix, content_matrix, asking_norm_gain, lookup_norm_gain, mixing_matrix, after_mixing_gain, before_hidden_gain, gating_matrix_entries, widening_matrix, lowering_matrix, after_hidden_gain, document_offsets):
    normed = narrow_number_format(quadratic_norm_apply(incoming_activations, before_mixing_gain))
    query_proj = low_back(jnp.dot(normed, asking_matrix, precision=highest))
    mapped_lookup_vectors = jnp.dot(normed, lookup_matrix, precision=highest)
    value_proj = jnp.dot(normed, content_matrix, precision=highest)
    queries = query_proj.reshape(TOKENS, HEADS, CHANNEL_COUNT).transpose(1, 0, 2)
    queries = narrow_number_format(angular_position_turn(quadratic_norm_apply(queries, asking_norm_gain), document_offsets))
    lookup_copies_each_group = low_back(jnp.broadcast_to(mapped_lookup_vectors[None], (HEADS, TOKENS, CHANNEL_COUNT)))
    lookup_copies_each_group = narrow_number_format(angular_position_turn(quadratic_norm_apply(lookup_copies_each_group, lookup_norm_gain), document_offsets))
    values_heads = narrow_number_format(low_back(jnp.broadcast_to(value_proj[None], (HEADS, TOKENS, CHANNEL_COUNT))))
    padding = jnp.zeros((HEADS, WINDOW, CHANNEL_COUNT), jnp.float32)
    keys_padded = jnp.concatenate([padding, lookup_copies_each_group], axis=1)
    values_padded = jnp.concatenate([padding, values_heads], axis=1)
    doc_start = jnp.arange(TOKENS, dtype=jnp.int32) - document_offsets

    def one_block(block_num):
        row_begin = block_num * WINDOW
        block_queries = lax.dynamic_slice_in_dim(queries, row_begin, WINDOW, 1)
        block_keys = lax.dynamic_slice_in_dim(keys_padded, row_begin, 2 * WINDOW, 1)
        block_values = lax.dynamic_slice_in_dim(values_padded, row_begin, 2 * WINDOW, 1)
        query_index = row_begin + jnp.arange(WINDOW, dtype=jnp.int32)
        key_index = row_begin - WINDOW + jnp.arange(2 * WINDOW, dtype=jnp.int32)
        starts = lax.dynamic_slice_in_dim(doc_start, row_begin, WINDOW, 0)
        scores = jnp.einsum('hqd,hkd->hqk', block_queries, block_keys, precision=highest) * CHANNEL_COUNT ** (-0.5)
        allowed = allowed_pairs(query_index, key_index, starts)
        scores = low_back(jnp.where(allowed[None], scores, big_negative))
        attention_probs = jax.nn.softmax(scores, axis=-1)
        return jnp.einsum('hqk,hkd->hqd', narrow_number_format(attention_probs), block_values, precision=highest)
    attended_blocks = lax.map(jax.checkpoint(one_block), jnp.arange(TOKENS // WINDOW, dtype=jnp.int32))
    mixed = attended_blocks.transpose(0, 2, 1, 3).reshape(TOKENS, HEADS * CHANNEL_COUNT)
    mixed = narrow_number_format(low_back(mixed))
    attended = low_back(jnp.dot(mixed, mixing_matrix, precision=highest))
    hidden = incoming_activations + quadratic_norm_apply(attended, after_mixing_gain)
    normed_mid = narrow_number_format(quadratic_norm_apply(hidden, before_hidden_gain))

    def feed_rows(row_block):
        return feed_block(row_block, gating_matrix_entries, widening_matrix, lowering_matrix)
    feed_out = lax.map(jax.checkpoint(feed_rows), normed_mid.reshape(TOKENS // TOK_REP, TOK_REP, D))
    feed_out = low_back(feed_out.reshape(TOKENS, D))
    return hidden + quadratic_norm_apply(feed_out, after_hidden_gain)

def reference(incoming_activations, document_offsets, before_mixing_gain, asking_matrix, lookup_matrix, content_matrix, asking_norm_gain, lookup_norm_gain, mixing_matrix, after_mixing_gain, before_hidden_gain, gating_matrix_entries, widening_matrix, lowering_matrix, after_hidden_gain, loss_sensitivity):
    as_single_precision = [incoming_activations, before_mixing_gain, asking_matrix, lookup_matrix, content_matrix, asking_norm_gain, lookup_norm_gain, mixing_matrix, after_mixing_gain, before_hidden_gain, gating_matrix_entries, widening_matrix, lowering_matrix, after_hidden_gain]
    as_single_precision = [array.astype(jnp.float32) for array in as_single_precision]
    result, pull_back = jax.vjp(partial(complete_decoder_block, document_offsets=document_offsets), *as_single_precision)
    gradients = pull_back(loss_sensitivity.astype(jnp.float32))
    return (result, gradients[0], gradients[1], gradients[2], gradients[3], gradients[4], gradients[5], gradients[6], gradients[7], gradients[8], gradients[9], gradients[10], gradients[11], gradients[12], gradients[13])
```

```python
import jax
import jax.numpy as jnp
import numpy as np
from jax import lax
from jax.experimental import pallas as pl
from jax.experimental.pallas import tpu as pltpu
from jax.sharding import PartitionSpec as P

WINDOW = 512
EPS = 1e-06
NEG = -1e30
ALL = ("group", "replica")
COUNT = 128
F32 = jnp.float32
BF16 = jnp.bfloat16

HI, CORE, LO = 64, 32, 16
PEER = HI | LO


def route(block, dest):
    return lax.ppermute(block, ALL, [(i, dest(i)) for i in range(COUNT)])


def flip(block, mask):
    return route(block, lambda i: i ^ mask)


def home_swap(block):
    return route(block, lambda i: i ^ LO if i & HI else i)


def block_of(i):
    return ((i >> 4 & 1) ^ (i >> 6 & 1)) * 16 + (i & 15)


def device_of(block, i):
    return (i & (HI | CORE)) | (((block >> 4) ^ (i >> 6)) & 1) * LO | (block & 15)


def to_block(value, step):
    pairs = [
        (i, device_of(block_of(i) + step, i))
        for i in range(COUNT)
        if 0 <= block_of(i) + step < 32
    ]
    return lax.ppermute(value, ALL, pairs)


def inv_rms(v):
    return lax.rsqrt(jnp.mean(v * v, axis=-1, keepdims=True) + EPS)


def rms_back(w, c, u, r):
    wc = w * c
    return r * (wc - u * jnp.mean(wc * u, axis=-1, keepdims=True))


def mm(a, b):
    return jnp.dot(a, b, preferred_element_type=F32)


def mm_t(a, b):
    return jnp.einsum("ik,jk->ij", a, b, preferred_element_type=F32)


def t_mm(a, b):
    return jnp.einsum("ki,kj->ij", a, b, preferred_element_type=F32)


def rope(v, cos, sin):
    h = v.shape[-1] // 2
    a, b = v[:, :h], v[:, h:]
    return jnp.concatenate([a * cos - b * sin, b * cos + a * sin], axis=-1)


def rope_back(w, cos, sin):
    h = w.shape[-1] // 2
    a, b = w[:, :h], w[:, h:]
    return jnp.concatenate([a * cos + b * sin, b * cos - a * sin], axis=-1)


def gather_rows(v):
    near = jnp.concatenate([v, flip(v, PEER)], axis=0)
    return near, flip(near, CORE)


def scatter_near(near_fn, far_fn):
    got = flip(far_fn().astype(BF16), CORE).astype(F32)
    total = near_fn() + got
    half = total.shape[0] // 2
    return total[:half], total[half:].astype(BF16)


def after(v, *others):
    for other in others:
        v = v + 0.0 * other.reshape(-1, other.shape[-1])[:1, :1].astype(v.dtype)
    return v


UNIT = 144
PART = 288
SPLIT = 896


def one_hot_rows(rows, size):
    return (rows[:, None] == jnp.arange(size, dtype=jnp.int32)[None, :]).astype(BF16)


def ring_rows(first, second, lo, z_first):
    at = np.arange(1152)
    unit, rest = at // UNIT, at % UNIT
    far = np.array([2, 1, 2, 3, 3, 1, 0, 0])[unit]
    half = np.array([0, 0, 1, 1, 0, 1, 0, 1])[unit]
    near = np.array([[0, 1], [2, 3]])[half, rest // 72]
    side = rest % 72 // 36
    one, two = first ^ far.astype(np.int32), second ^ near.astype(np.int32)
    z, y = (one, two) if z_first else (two, one)
    chunk = (lo ^ side.astype(np.int32)) * 16 + z * 4 + y
    return chunk * 36 + (rest % 36).astype(np.int32)


def never(other):
    return (0.0 * other[0, 0].astype(F32)).astype(jnp.int32)


def add(*parts):
    total = parts[0].astype(F32)
    for part in parts[1:]:
        total = total + part.astype(F32)
    return total


def ring_first(near, far, first):
    return flip(near, 1 << first), flip(far, 3 << first)


def ring_second(turn, got, first, wait):
    n = UNIT
    got_near, got_far = got
    to_far = after(add(turn[:n], got_near[:n]), *wait).astype(BF16)
    to_near = after(add(turn[n:], got_far[:n]), *wait).astype(BF16)
    return flip(to_far, 3 << first), flip(to_near, 1 << first)


def ring_third(own, got, back, wait):
    n, h = UNIT, UNIT // 2
    low = [own[:n], got[0][n:], back[0]]
    high = [own[n:], got[1][n:], back[1]]
    return [
        after(add(*[v[at : at + h] for v in some]), *wait).astype(BF16)
        for some in (low, high)
        for at in (0, h)
    ]


def stage4(parts, shift):
    return add(parts[0], *[flip(parts[j], j << shift) for j in (1, 2, 3)])


def split(v, count):
    n = v.shape[0] // count
    return [v[j * n : (j + 1) * n] for j in range(count)]


def stage2(parts, mask):
    return add(parts[0], flip(parts[1], mask))


NT = (((1,), (1,)), ((), ()))


def grad_kernel(first, a1, b1, a2, b2, _, one, two):
    def part(a, b):
        return lax.dot_general(a, b, NT, preferred_element_type=F32).astype(BF16)

    def fill(out):
        out[:, :SPLIT] = part(a1[...], b1[first : first + SPLIT])
        out[:, SPLIT:] = part(a2[...], b2[...])

    step = pl.program_id(0)
    pl.when(step == 0)(lambda: fill(one))
    pl.when(step == 1)(lambda: fill(two))


def grad_rows(a1, b1, first, a2, b2, start, wait):
    depth = a1.shape[1]
    cols = SPLIT + b2.shape[0]

    def whole(rows, width):
        return pl.BlockSpec((rows, width), lambda i: (0, 0))

    some = pl.BlockSpec((PART, depth), lambda i: (start + i, 0))
    shape = jax.ShapeDtypeStruct((PART, cols), BF16)
    return pl.pallas_call(
        lambda *refs: grad_kernel(first, *refs),
        grid=(2,),
        in_specs=[
            some,
            whole(*b1.shape),
            some,
            whole(*b2.shape),
            pl.BlockSpec(memory_space=pl.ANY),
        ],
        out_specs=[whole(PART, cols)] * 2,
        out_shape=[shape] * 2,
        compiler_params=pltpu.CompilerParams(vmem_limit_bytes=40 * 2**20),
        cost_estimate=pl.CostEstimate(
            flops=4 * PART * cols * depth,
            bytes_accessed=2 * (2 * PART * cols + 4 * PART * depth + 2 * b2.size),
            transcendentals=0,
        ),
    )(a1, b1, a2, b2, wait)


def pair_kernel(a1, b1, a2, b2, a3, a4, small, out):
    width = b1.shape[1]
    rows3, rows4 = a3[...], a4[...]
    out[:, :width] = (mm(a1[...], b1[...]) + mm(rows3, small[:, :width])).astype(BF16)
    out[:, width:] = (
        mm(a2[...], b2[...]) + mm(rows3, small[:, width : 2 * width])
    ).astype(BF16)
    gains = mm(rows4, small[:, 2 * width :]) + out[:, :128].astype(F32)
    out[:, :128] = gains.astype(BF16)


def small_kernel(a1, b1, cols, *outs):
    n = a1.shape[0] // len(outs)
    width = b1.shape[1]
    for j, out in enumerate(outs):
        rows = slice(j * n, (j + 1) * n)
        out[:, :width] = mm(a1[rows], b1[...]).astype(BF16)
        out[:, width:] = cols[rows].astype(BF16)


def in_parts(kernel, count, cols, *args):
    rows = args[0].shape[0]
    shape = jax.ShapeDtypeStruct((rows // count, cols), BF16)
    return pl.pallas_call(
        kernel,
        out_shape=[shape] * count,
        compiler_params=pltpu.CompilerParams(vmem_limit_bytes=32 * 2**20),
        cost_estimate=pl.CostEstimate(
            flops=2 * rows * cols * 512, bytes_accessed=5 * 2**20, transcendentals=0
        ),
    )(*args)


def per_device(
    incoming_activations,
    document_offsets,
    before_mixing_gain,
    asking_matrix,
    lookup_matrix,
    content_matrix,
    asking_norm_gain,
    lookup_norm_gain,
    mixing_matrix,
    after_mixing_gain,
    before_hidden_gain,
    gating_matrix_entries,
    widening_matrix,
    lowering_matrix,
    after_hidden_gain,
    loss_sensitivity,
):
    group = lax.axis_index("group")
    replica = lax.axis_index("replica")
    upper = group >= 2
    block = ((replica >> 4) ^ (group >> 1)) * 16 + (replica & 15)
    width = 256
    factor = width ** (-0.5)

    lo, z, y = replica >> 4, replica >> 2 & 3, replica & 3
    x = home_swap(incoming_activations).astype(F32)
    offsets = home_swap(document_offsets.astype(F32)).astype(jnp.int32)

    order = jnp.stack([group, group ^ 2, group ^ 1, group ^ 3])
    lane = jnp.arange(128, dtype=jnp.int32)
    token = (block * 512 + order[:, None] * 128 + lane[None, :]).reshape(512)
    places = jnp.take(offsets.reshape(4, 128), order, axis=0).reshape(512)
    doc_start = token - places
    inverse = 10000.0 ** (-2.0 * jnp.arange(width // 2, dtype=F32) / width)
    angles = places.astype(F32)[:, None] * inverse[None, :]
    cos, sin = jnp.cos(angles), jnp.sin(angles)

    r1 = inv_rms(x)
    u1 = x * r1
    near, far = gather_rows((u1 * before_mixing_gain).astype(BF16))
    normed = jnp.concatenate([near, far], axis=0)
    kv_matrix = jnp.concatenate([lookup_matrix, content_matrix], axis=1)
    kv_proj = mm(normed, kv_matrix)
    k_proj = kv_proj[:, :width]
    rk = inv_rms(k_proj)
    uk = k_proj * rk
    keys = rope(uk * lookup_norm_gain, cos, sin).astype(BF16)
    values = kv_proj[:, width:].astype(BF16)
    g = home_swap(loss_sensitivity).astype(F32)
    kv = after(jnp.concatenate([keys, values], axis=1), g)
    before_near = to_block(kv[:256], 1)
    before_far = flip(before_near, CORE)
    before = jnp.concatenate([before_near, before_far], axis=0)
    before_keys, before_values = before[:, :width], before[:, width:]

    q_proj = mm(normed, asking_matrix)
    rq = inv_rms(q_proj)
    uq = q_proj * rq
    queries = rope(uq * asking_norm_gain, cos, sin).astype(BF16)

    chunk, row = np.divmod(np.arange(32 * 56, dtype=np.int32), 56)
    pair_at = jnp.asarray(np.where(row < 36, chunk * 36 + row, -1))
    kv_at = jnp.asarray(np.where((row >= 36) & (row < 45), chunk * 9 + row - 36, -1))
    gains_at = jnp.asarray(np.where((row >= 45) & (row < 54), chunk * 9 + row - 45, -1))
    rows_pair = one_hot_rows(pair_at + never(kv), 1152)
    normed_pair = mm_t(rows_pair, normed).astype(BF16)

    at = np.arange(1152, dtype=np.int32)
    device = (
        ((group >> 1) ^ (at // 288 & 1)) * 64
        + ((group & 1) ^ (at // 576)) * 32
        + at // 9 % 32
    )

    def scores(some_keys, key_token):
        allowed = (
            (key_token[None, :] <= token[:, None])
            & (key_token[None, :] > token[:, None] - WINDOW)
            & (key_token[None, :] >= doc_start[:, None])
        )
        return jnp.where(allowed, mm_t(queries, some_keys) * factor, NEG)

    s_own = scores(keys, token)
    s_before = after(scores(before_keys, token - 512), normed_pair)
    peak = jnp.maximum(
        jnp.max(s_own, axis=1, keepdims=True), jnp.max(s_before, axis=1, keepdims=True)
    )
    e_own, e_before = jnp.exp(s_own - peak), jnp.exp(s_before - peak)
    inv_sum = 1.0 / (
        jnp.sum(e_own, axis=1, keepdims=True) + jnp.sum(e_before, axis=1, keepdims=True)
    )
    p_own, p_before = e_own * inv_sum, e_before * inv_sum
    p_own_low, p_before_low = p_own.astype(BF16), p_before.astype(BF16)
    mixed = (mm(p_own_low, values) + mm(p_before_low, before_values)).astype(BF16)
    attended_own, to_peer = scatter_near(
        lambda: mm(mixed[:256], mixing_matrix), lambda: mm(mixed[256:], mixing_matrix)
    )
    rows_small = one_hot_rows(device * 9 + at % 9 + never(to_peer), 1152)
    normed_small = mm_t(rows_small, normed).astype(BF16)
    attended = after(add(attended_own, flip(to_peer, PEER)), normed_small)

    r2 = inv_rms(attended)
    u2 = attended * r2
    hidden = x + u2 * after_mixing_gain
    r3 = inv_rms(hidden)
    u3 = hidden * r3
    inner_near, inner_far = gather_rows((u3 * before_hidden_gain).astype(BF16))

    def feed(rows):
        gate = mm(rows, gating_matrix_entries)
        up = mm(rows, widening_matrix)
        active, pull = jax.vjp(lambda a, b: jax.nn.gelu(a, approximate=True) * b, gate, up)
        return active.astype(BF16), pull

    active_near, pull_near = feed(inner_near)
    active_far, pull_far = feed(inner_far)
    fed_own, to_peer = scatter_near(
        lambda: mm(active_near, lowering_matrix), lambda: mm(active_far, lowering_matrix)
    )
    fed = add(fed_own, flip(to_peer, PEER))

    r4 = inv_rms(fed)
    u4 = fed * r4
    block_out = hidden + u4 * after_hidden_gain
    fed_bar = rms_back(g, after_hidden_gain, u4, r4).astype(BF16)
    closing_part = jnp.sum(g * u4, axis=0)
    inner = jnp.concatenate([inner_near, inner_far], axis=0)
    order_z = ring_rows(z, y, lo, True) + never(fed_bar)
    order_y = ring_rows(y, z, lo, False) + never(fed_bar)
    rows_z, rows_y = one_hot_rows(order_z, 1152), one_hot_rows(order_y, 1152)
    inner_z = mm_t(rows_z, inner).astype(BF16)
    inner_y = mm_t(rows_y, inner).astype(BF16)
    fed_near, fed_far = gather_rows(fed_bar)

    def feed_back(rows, pull, wait):
        gate_bar, up_bar = pull(after(mm_t(rows, lowering_matrix), *wait))
        gate_low, up_low = gate_bar.astype(BF16), up_bar.astype(BF16)
        return gate_low, up_low

    gate_near, up_near = feed_back(fed_near, pull_near, [inner_z, inner_y])
    gate_far, up_far = feed_back(fed_far, pull_far, [])

    def inner_part_of(gate_low, up_low):
        return mm_t(gate_low, gating_matrix_entries) + mm_t(up_low, widening_matrix)

    inner_own, inner_send = scatter_near(
        lambda: inner_part_of(gate_near, up_near), lambda: inner_part_of(gate_far, up_far)
    )
    inner_bar = add(inner_own, flip(inner_send, PEER))
    fed_all = jnp.concatenate([fed_near, fed_far], axis=0)
    active_t = jnp.concatenate([active_near, active_far], axis=0).T
    gate_t = jnp.concatenate([gate_near, gate_far], axis=0).T
    up_t = jnp.concatenate([up_near, up_far], axis=0).T
    rows_z = one_hot_rows(order_z + never(inner_send), 1152)
    fed_z = mm_t(rows_z, fed_all).astype(BF16)
    args_z = inner_z, up_t, 0, fed_z, active_t
    args_y = inner_y, up_t, 1728 - SPLIT, inner_y, gate_t
    first_z = grad_rows(*args_z, 0, inner_send)
    first_y = grad_rows(*args_y, 0, inner_send)
    got_z, got_y = ring_first(*first_z, 2), ring_first(*first_y, 0)

    inner_grad_part = jnp.sum(inner_bar * u3, axis=0)
    hidden_bar = g + rms_back(inner_bar, before_hidden_gain, u3, r3)
    attend_part = jnp.sum(hidden_bar * u2, axis=0)
    attended_bar = rms_back(hidden_bar, after_mixing_gain, u2, r2)
    attended_bar = after(attended_bar, first_z[0], first_y[0]).astype(BF16)
    att_near, att_far = gather_rows(attended_bar)
    attended_all = jnp.concatenate([att_near, att_far], axis=0)
    mixed_bar = mm_t(attended_all, mixing_matrix).astype(BF16)
    dp_own = mm_t(mixed_bar, values)
    dp_before = mm_t(mixed_bar, before_values)
    delta = jnp.sum(p_own * dp_own, axis=1, keepdims=True) + jnp.sum(
        p_before * dp_before, axis=1, keepdims=True
    )
    ds_own = (p_own * (dp_own - delta)).astype(BF16)
    ds_before = (p_before * (dp_before - delta)).astype(BF16)
    edge = jnp.concatenate(
        [t_mm(ds_before, queries) * factor, t_mm(p_before_low, mixed_bar)], axis=1
    )
    edge_near = edge[:256] + flip(edge[256:].astype(BF16), CORE).astype(F32)
    edge_send = edge_near.astype(BF16)
    edge_in = to_block(edge_send, -1).astype(F32)
    q_bar = (mm(ds_own, keys) + mm(ds_before, before_keys)) * factor
    k_bar = t_mm(ds_own, queries) * factor
    v_bar = t_mm(p_own_low, mixed_bar)
    wq = rope_back(q_bar, cos, sin)
    qscale_part = jnp.sum(wq * uq, axis=0)
    q_low = rms_back(wq, asking_norm_gain, uq, rq).astype(BF16)
    turn_z, own_z = grad_rows(*args_z, 2, edge_send)
    turn_y, own_y = grad_rows(*args_y, 2, edge_send)
    back_z = ring_second(turn_z, got_z, 2, [edge_send])
    back_y = ring_second(turn_y, got_y, 0, [edge_send])
    rows_home = home_swap(
        after(jnp.concatenate([hidden_bar, block_out], axis=0), edge_send).astype(BF16)
    )
    hidden_bar_home = jnp.where(upper, rows_home[:128].astype(F32), hidden_bar)
    block_out = jnp.where(upper, rows_home[128:].astype(F32), block_out)
    k_bar = jnp.concatenate([k_bar[:256] + edge_in[:, :width], k_bar[256:]], axis=0)
    v_bar = jnp.concatenate([v_bar[:256] + edge_in[:, width:], v_bar[256:]], axis=0)
    wk = rope_back(k_bar, cos, sin)
    kscale_part = jnp.sum(wk * uk, axis=0)
    kv_low = jnp.concatenate(
        [rms_back(wk, lookup_norm_gain, uk, rk).astype(BF16), v_bar.astype(BF16)], axis=1
    )

    entry = []

    def normed_part(rows):
        part = mm_t(q_low[rows], asking_matrix) + mm_t(kv_low[rows], kv_matrix)
        entry.append(jnp.sum(part * normed[rows].astype(F32), axis=0))
        return part

    bar_own, bar_send = scatter_near(
        lambda: normed_part(slice(0, 256)), lambda: normed_part(slice(256, 512))
    )
    bar_peer = route(bar_send, lambda i: i ^ PEER if i & HI else i ^ HI)
    bar_home = home_swap(bar_own.astype(BF16))
    entry_part = (entry[0] + entry[1]) / before_mixing_gain

    rows_scale = one_hot_rows(jnp.where(at % 9 < 2, device * 2 + at % 9, -1), 256)
    gains = jnp.stack([entry_part, attend_part, inner_grad_part, closing_part])
    scales = jnp.stack([qscale_part, kscale_part])
    gains = jnp.pad(gains, ((0, 124), (0, 0))).astype(BF16)
    scales = jnp.pad(scales, ((4, 122), (0, 0))).astype(BF16)
    gains = mm_t(rows_small, gains) + mm_t(rows_scale, scales)
    small = in_parts(small_kernel, 2, 640, normed_small, kv_low, gains)
    small = stage2(small, CORE).astype(BF16)
    small_own, small_send = split(small, 2)
    small = add(small_own, flip(small_send, PEER)).astype(BF16)
    last_z = ring_third(own_z, got_z, back_z, [bar_send])
    last_y = ring_third(own_y, got_y, back_y, [bar_home, bar_peer, small_send])
    rows_pair = one_hot_rows(pair_at + never(bar_send), 1152)
    attended_pair = mm_t(rows_pair, attended_all).astype(BF16)
    (both,) = in_parts(
        pair_kernel,
        1,
        512,
        normed_pair,
        q_low,
        attended_pair,
        mixed,
        one_hot_rows(kv_at, 288),
        one_hot_rows(gains_at, 288),
        after(small, bar_peer).astype(BF16),
    )
    last_z = after(stage4(last_z, 0), both).astype(BF16)
    both = lax.all_to_all(both.reshape(32, 56, 512), "replica", 0, 0)
    both = jnp.sum(both.astype(F32), axis=0)
    last_y = after(stage4(last_y, 2), both).astype(BF16)
    pair, kv_sum, gain_sum = both[:36], both[36:45], both[45:54]
    own_half, send_half = split(jnp.concatenate([last_z, last_y], axis=1), 2)
    sums = add(own_half, flip(send_half, LO))
    sum_z, sum_y = sums[:, : SPLIT + 1728], sums[:, SPLIT + 1728 :]
    down_sum, gate_sum = sum_z[:, SPLIT:], sum_y[:, SPLIT:]
    up_sum = jnp.concatenate(
        [sum_z[:, :SPLIT], sum_y[:, 2 * SPLIT - 1728 : SPLIT]], axis=1
    )

    x_home = incoming_activations.astype(F32)
    r_home = inv_rms(x_home)
    tokens = hidden_bar_home + rms_back(
        add(bar_peer, bar_home), before_mixing_gain, x_home * r_home, r_home
    )

    return (
        block_out,
        tokens,
        gain_sum[:, 0],
        pair[:, :256],
        kv_sum[:, :256],
        kv_sum[:, 256:],
        gain_sum[:2, 4],
        gain_sum[:2, 5],
        pair[:, 256:].T,
        gain_sum[:, 1],
        gain_sum[:, 2],
        gate_sum,
        up_sum,
        down_sum.T,
        gain_sum[:, 3],
    )


def solution(mesh):
    in_specs = (
        P(("replica", "group"), None),
        P("replica"),
        P(),
        P(None, "group"),
        P(),
        P(),
        P(),
        P(),
        P("group", None),
        P(),
        P(),
        P(None, "group"),
        P(None, "group"),
        P("group", None),
        P(),
        P(("replica", "group"), None),
    )
    out_specs = (
        P(("replica", "group"), None),
        P(("replica", "group"), None),
        P(("group", "replica")),
        P("replica", "group"),
        P(("group", "replica"), None),
        P(("group", "replica"), None),
        P(("group", "replica")),
        P(("group", "replica")),
        P("group", "replica"),
        P(("group", "replica")),
        P(("group", "replica")),
        P("replica", "group"),
        P("replica", "group"),
        P("group", "replica"),
        P(("group", "replica")),
    )
    return jax.shard_map(
        per_device, mesh=mesh, in_specs=in_specs, out_specs=out_specs, check_vma=False
    )
```
